32 devices in a mesh: dp: 2 (over core), expert: 4 (over y, x), tensor: 4 (over z).
Axes of the slice: x: 2, y: 2, z: 4, core: 2. Of those that a mesh axis runs over, the one named last changes fastest.
Arguments:
- out_grad: bfloat16 [2, 512, 6144], P('dp', ('expert', 'tensor')), may hold values from -4 to 4
- routes: int32 [2, 512, 2], P('dp', ('expert', 'tensor')), may hold values from 0 to 3, all different within a row; in each aligned block of 32 rows (0 to 31, 32 to 63, ..., all dimensions but the last counted through in order) at most 32 rows name the same one
- route_weight: bfloat16 [2, 512, 2], P('dp', ('expert', 'tensor')), may hold values from 0.19921875 to 0.796875
- gate_pre: bfloat16 [2, 4, 512, 8192], P('dp', 'expert', None, 'tensor'), may hold values from -8 to 8
- up_pre: bfloat16 [2, 4, 512, 8192], P('dp', 'expert', None, 'tensor'), may hold values from -6 to 6
- down_weight: bfloat16 [4, 8192, 6144], P('expert', 'tensor', 'dp'), may hold values from -0.0625 to 0.0625
Outputs:
- route_grad: float32 [2, 512, 2], P('dp', ('expert', 'tensor'))
- gate_grad: bfloat16 [2, 4, 512, 8192], P('dp', 'expert', None, 'tensor')
- up_grad: bfloat16 [2, 4, 512, 8192], P('dp', 'expert', None, 'tensor')
- down_grad: bfloat16 [4, 8192, 6144], P('expert', 'tensor', 'dp')
The draws below stay inside these ranges and needn't reach their ends.
Inputs may be any that keep to these rules, and one draw needn't show every extreme that they name: `routes`: the two experts of a token differ. Among the tokens of one shard (32 tokens in a row, aligned) no expert is named more than 32 times, and in every draw some expert is named exactly 32 times by the tokens of some shard.
All inputs are finite; a program needn't handle non-finite values.
Results may differ from the reference program's by a relative error of at most 0.008.
Values may be sent and summed in bfloat16 or wider, within the bound.
A program may use at most 128 MiB of HBM per device.

```python
import math
import jax
import jax.numpy as jnp
import numpy as np
from jax import lax

D = 6144
FF = 8192
TOK_DEV = 32
EXPERTS = 4
TOKENS = 512
CAP = 32
ROWS = 512
N_DP = 2
N_EXPERT = 4
N_TENSOR = 4


def steps_of(stream_key, dims, pieces, least, high):
    gain = 1.0
    for dim, parts in pieces:
        steps = jax.random.uniform(jax.random.fold_in(jax.random.fold_in(stream_key, 6), dim), (parts,), jnp.float32, least / len(pieces), high / len(pieces))
        gain = gain * jnp.repeat(jnp.exp(steps), dims[dim] // parts).reshape((-1,) + (1,) * (len(dims) - 1 - dim))
    return gain


def assign_block(stream_key, own, number, rows, amount, top, reach, lean):
    sequence = jax.random.permutation(stream_key, amount)
    packed, common = load_shares(amount, rows * top, reach, lean, True), load_shares(amount, rows * top, reach, lean, False)
    places = jnp.arange(amount)

    def named(sizes, rotation):
        used = int((sizes > 0).sum())
        fixed = max(1, used // 4)
        shifted = fixed + (places - fixed + rotation * (used - fixed)) % max(1, amount - fixed)
        return jnp.zeros((amount,), jnp.int32).at[sequence[jnp.where(places < fixed, places, shifted)]].set(jnp.asarray(sizes, jnp.int32))

    sizes = jnp.where(number % 4 == 0, named(packed, number // 4), named(common, number - number // 4 - 1))
    mixed = jax.random.permutation(jax.random.fold_in(own, 3), amount)
    giver, sink = mixed[0:amount // 2 * 2:2], mixed[1:amount // 2 * 2:2]
    room = jnp.minimum(sizes[giver] - 1, reach - sizes[sink]) // 2
    room = jnp.where((giver == sequence[0]) | (sink == sequence[0]) | (sizes[sink] == 0), 0, jnp.maximum(room, 0))
    shifted = jax.random.randint(jax.random.fold_in(own, 4), (amount // 2,), 0, 1 << 20) % (room + 1)
    sizes = sizes.at[giver].add(-shifted).at[sink].add(shifted)
    items = jnp.searchsorted(jnp.cumsum(sizes), jnp.arange(rows * top), side="right").astype(jnp.int32)
    listing = items.reshape(top, rows).T
    listing = listing[jax.random.permutation(jax.random.fold_in(own, 1), rows)]
    rotation = jax.random.randint(jax.random.fold_in(own, 2), (rows, 1), 0, top)
    return jnp.take_along_axis(listing, (jnp.arange(top)[None, :] + rotation) % top, axis=1)


def load_shares(amount, total, reach, skew, full):
    loads = [(1 << 20) // math.isqrt(grade ** skew) + 1 for grade in range(1, amount + 1)]
    largest = reach if full else min(reach, max(-(-total // amount), total * loads[0] // sum(loads)))
    least = 1 if total - largest >= amount - 1 else 0
    given, rest = [largest] + [least] * (amount - 1), total - largest - least * (amount - 1)
    while rest > 0:
        movable = [i for i in range(1, amount) if given[i] < largest] or [i for i in range(1, amount) if given[i] < reach]
        mass, remaining = sum([loads[i] for i in movable]), rest
        for i in movable:
            addition = min(reach - given[i], max(1, remaining * loads[i] // mass), rest)
            given[i] = given[i] + addition
            rest = rest - addition
    return np.array(given)


def gaussian(own_key, dims, deviation, bound, split=(), kind=jnp.bfloat16):
    drawn = deviation * jax.random.normal(own_key, dims, jnp.float32)
    if split:
        drawn = drawn * steps_of(own_key, dims, split, -0.22, 0.18)
    return jnp.clip(drawn, -bound, bound).astype(kind)


def setup_inputs(seed: int = 0) -> dict:
    seeds = jax.random.split(jax.random.key(seed), 7)
    out_grad = gaussian(seeds[0], (N_DP, TOKENS, D), 0.5, 4.0, ((0, 2), (1, 16)))
    routes_keys = jax.random.split(jax.random.fold_in(seeds[1], 1), N_DP * TOKENS // TOK_DEV)
    routes_turns = jax.random.permutation(jax.random.fold_in(seeds[1], 3), N_DP * TOKENS // TOK_DEV)
    routes = jax.vmap(lambda own, number: assign_block(jax.random.fold_in(seeds[1], 2), own, number, TOK_DEV, EXPERTS, 2, CAP, 2))(routes_keys, routes_turns).reshape((N_DP, TOKENS, 2))
    route_weight = jnp.clip(0.19921875 + 0.59765625 * jax.random.uniform(seeds[2], (N_DP, TOKENS, 2), jnp.float32) ** steps_of(seeds[2], (N_DP, TOKENS, 2), ((0, 2), (1, 16)), -0.2, 0.2), 0.19921875, 0.796875).astype(jnp.bfloat16)
    gate_pre = gaussian(seeds[3], (N_DP, EXPERTS, ROWS, FF), 1.5, 8.0, ((0, 2), (1, 4), (3, 4)))
    up_pre = gaussian(seeds[4], (N_DP, EXPERTS, ROWS, FF), 1.0, 6.0, ((0, 2), (1, 4), (3, 4)))
    down_weight = gaussian(seeds[5], (EXPERTS, FF, D), FF ** -0.5, 0.0625, ((0, 4), (1, 4), (2, 2)))
    return dict(out_grad=out_grad, routes=routes, route_weight=route_weight, gate_pre=gate_pre, up_pre=up_pre, down_weight=down_weight)


def silu_parts(gate):
    sig = jax.nn.sigmoid(gate)
    return gate * sig, sig * (1.0 + gate * (1.0 - sig))


def reference(out_grad, routes, route_weight, gate_pre, up_pre, down_weight):
    shards = N_EXPERT * N_TENSOR
    flat = routes.reshape(N_DP, shards, TOK_DEV * 2).astype(jnp.int32)
    onehot = (flat[..., None] == jnp.arange(EXPERTS, dtype=jnp.int32)).astype(jnp.int32)
    position = jnp.cumsum(onehot, axis=2) - 1
    slot = jnp.sum(onehot * position, axis=3).astype(jnp.int32)
    row = jnp.arange(shards, dtype=jnp.int32)[None, :, None] * CAP + slot
    dest = (flat * ROWS + row).reshape(N_DP, shards * TOK_DEV * 2).astype(jnp.int32)
    group = jnp.arange(N_DP, dtype=jnp.int32)[:, None]
    pair_grad = jnp.repeat(out_grad, 2, axis=1)
    pair_weight = route_weight.reshape(N_DP, TOKENS * 2)
    routed_grad = jnp.zeros((N_DP, EXPERTS * ROWS, D), jnp.bfloat16).at[group, dest].set(pair_grad)
    routed_weight = jnp.zeros((N_DP, EXPERTS * ROWS), jnp.bfloat16).at[group, dest].set(pair_weight)
    routed_grad = jnp.swapaxes(routed_grad.reshape(N_DP, EXPERTS, ROWS, D), 0, 1)
    routed_weight = jnp.swapaxes(routed_weight.reshape(N_DP, EXPERTS, ROWS), 0, 1)

    def one_expert(items):
        grads, weights, gates, uppers, weight = items
        gate_out, up_out, score_out = [], [], []
        total = jnp.zeros((FF, D), jnp.float32)
        for batch in range(N_DP):
            gate = gates[batch].astype(jnp.float32)
            upper = uppers[batch].astype(jnp.float32)
            act, slope = silu_parts(gate)
            hidden = (act * upper).astype(jnp.bfloat16)
            back = jnp.dot(grads[batch], weight.T, preferred_element_type=jnp.float32)
            scale = weights[batch].astype(jnp.float32)[:, None]
            hidden_grad = scale * back
            gate_out.append((hidden_grad * upper * slope).astype(jnp.bfloat16))
            up_out.append((hidden_grad * act).astype(jnp.bfloat16))
            scaled = (scale * grads[batch].astype(jnp.float32)).astype(jnp.bfloat16)
            part = jnp.dot(hidden.T, scaled, preferred_element_type=jnp.float32).astype(jnp.bfloat16)
            total = total + part.astype(jnp.float32)
            score_out.append(jnp.sum(hidden.astype(jnp.float32) * back, axis=1))
        return jnp.stack(gate_out), jnp.stack(up_out), total.astype(jnp.bfloat16), jnp.stack(score_out)

    gate_grad, up_grad, down_grad, score = lax.map(
        one_expert,
        (routed_grad, routed_weight, jnp.swapaxes(gate_pre, 0, 1), jnp.swapaxes(up_pre, 0, 1), down_weight))
    gate_grad = jnp.swapaxes(gate_grad, 0, 1)
    up_grad = jnp.swapaxes(up_grad, 0, 1)
    score = jnp.swapaxes(score, 0, 1).reshape(N_DP, EXPERTS * ROWS)
    route_grad = score[group, dest].reshape(N_DP, TOKENS, 2)
    return route_grad, gate_grad, up_grad, down_grad
```

```python
import jax
import jax.numpy as jnp
from jax import lax
from jax.sharding import PartitionSpec as P

BF = jnp.bfloat16
F32 = jnp.float32


def swap(x):
    return lax.ppermute(x, "dp", [(0, 1), (1, 0)])


def shards(out_grad, routes, route_weight, gate_pre, up_pre, down_weight):
    me = lax.axis_index("dp")
    expert = lax.axis_index("expert")
    n = lax.axis_size("expert") * lax.axis_size("tensor")
    rows = gate_pre.shape[2]
    cap = rows // n
    tok, width = out_grad.shape[1:]
    half = width // 2
    first = me == 0

    def ordered(mine, other):
        return jnp.where(first, mine, other), jnp.where(first, other, mine)

    meta = jnp.concatenate([routes[0].T.astype(F32), route_weight[0].T.astype(F32)], axis=0)
    meta = lax.all_gather(meta, ("dp", "expert", "tensor"), axis=0)
    meta = meta.reshape(2, n, 4, tok)

    low, high = out_grad[0, :, :half], out_grad[0, :, half:]
    keep = jnp.where(first, low, high)
    other = swap(jnp.where(first, high, low))
    both = jnp.stack(ordered(keep, other))
    tokens = lax.all_gather(both, ("expert", "tensor"), axis=1)

    hits = meta[:, :, :2] == expert.astype(F32)
    taken = jnp.any(hits, axis=2)
    before = jnp.arange(tok)[:, None] > jnp.arange(tok)[None, :]
    slot = jnp.sum(jnp.where(taken[:, :, None, :] & before, 1, 0), axis=3)
    place = taken[:, :, None, :] & (slot[:, :, None, :] == jnp.arange(cap)[:, None])
    tok_weight = jnp.sum(jnp.where(hits, meta[:, :, 2:], 0.0), axis=2)
    scale = jnp.sum(jnp.where(place, tok_weight[:, :, None, :], 0.0), axis=3)
    scale = scale.reshape(2 * rows, 1)

    group = max(1, min(n, 256 // tok))
    eye = jnp.eye(group, dtype=bool)
    wide = place.reshape(2, n // group, group, cap, 1, tok) & eye[:, None, :, None]
    wide = wide.reshape(2 * n // group, group * cap, group * tok).astype(BF)
    routed = lax.dot_general(
        wide,
        tokens.reshape(2 * n // group, group * tok, half),
        (((2,), (1,)), ((0,), (0,))),
        preferred_element_type=F32,
    ).reshape(2 * rows, half)
    routed = routed.astype(BF)

    gate = gate_pre[0, 0].astype(F32)
    upper = up_pre[0, 0].astype(F32)
    sig = jax.nn.sigmoid(gate)
    act = gate * sig
    slope = sig * (1.0 + gate * (1.0 - sig))
    hidden = (act * upper).astype(BF)
    hidden_both = jnp.concatenate(ordered(hidden, swap(hidden)), axis=0)

    back = lax.dot_general(
        routed, down_weight[0], (((1,), (1,)), ((), ())), preferred_element_type=F32
    ).reshape(2, rows, -1)
    sent = lax.dynamic_index_in_dim(back, 1 - me, 0, keepdims=False).astype(BF)
    back = lax.dynamic_index_in_dim(back, me, 0, keepdims=False) + swap(sent).astype(F32)

    scaled = (scale * routed).astype(BF)
    down_grad = lax.dot_general(
        hidden_both, scaled, (((0,), (0,)), ((), ())), preferred_element_type=F32
    ).astype(BF)

    my_scale = lax.dynamic_slice_in_dim(scale, me * rows, rows, 0)
    hidden_grad = my_scale * back
    gate_grad = (hidden_grad * upper * slope).astype(BF)
    up_grad = (hidden_grad * act).astype(BF)
    score = jnp.sum(hidden.astype(F32) * back, axis=1).reshape(n, cap, 1)
    my_place = lax.dynamic_index_in_dim(place, me, 0, keepdims=False)
    my_hits = lax.dynamic_index_in_dim(hits, me, 0, keepdims=False)
    tok_score = jnp.sum(jnp.where(my_place, score, 0.0), axis=1)
    pair = jnp.where(my_hits, tok_score[:, None, :], 0.0)
    pair = lax.psum_scatter(pair, ("expert", "tensor"), scatter_dimension=0, tiled=True)
    route_grad = pair.reshape(2, tok).T[None]
    return (route_grad, gate_grad[None, None], up_grad[None, None], down_grad[None])


def solution(mesh):
    in_specs = (
        P("dp", ("expert", "tensor"), None),
        P("dp", ("expert", "tensor"), None),
        P("dp", ("expert", "tensor"), None),
        P("dp", "expert", None, "tensor"),
        P("dp", "expert", None, "tensor"),
        P("expert", "tensor", "dp"),
    )
    out_specs = (
        P("dp", ("expert", "tensor"), None),
        P("dp", "expert", None, "tensor"),
        P("dp", "expert", None, "tensor"),
        P("expert", "tensor", "dp"),
    )
    return jax.shard_map(shards, mesh=mesh, in_specs=in_specs, out_specs=out_specs, check_vma=False)
```

```python
import jax
import jax.numpy as jnp
from jax import lax
from jax.sharding import PartitionSpec as P

BF = jnp.bfloat16
F32 = jnp.float32


def swap(x):
    return lax.ppermute(x, "dp", [(0, 1), (1, 0)])


def shards(out_grad, routes, route_weight, gate_pre, up_pre, down_weight):
    me = lax.axis_index("dp")
    expert = lax.axis_index("expert")
    n = lax.axis_size("expert") * lax.axis_size("tensor")
    rows = gate_pre.shape[2]
    cap = rows // n
    tok, width = out_grad.shape[1:]
    half = width // 2
    first = me == 0

    def ordered(mine, other):
        return jnp.where(first, mine, other), jnp.where(first, other, mine)

    meta = jnp.concatenate([routes[0].T.astype(F32), route_weight[0].T.astype(F32)], axis=0)
    meta = jnp.stack(ordered(meta, swap(meta)))
    meta = jnp.broadcast_to(meta[None], (n, 2, 4, tok))
    meta = lax.all_to_all(meta, ("expert", "tensor"), split_axis=0, concat_axis=0, tiled=True)
    meta = jnp.swapaxes(meta, 0, 1)

    low, high = out_grad[0, :, :half], out_grad[0, :, half:]
    keep = jnp.where(first, low, high)
    other = swap(jnp.where(first, high, low))
    both = jnp.stack(ordered(keep, other))
    piece = half // 2
    tokens_a = lax.all_gather(both[:, :, :piece], ("expert", "tensor"), axis=1)
    later, tokens_a = lax.optimization_barrier((both[:, :, piece:], tokens_a))
    tokens_b = lax.all_gather(later, ("expert", "tensor"), axis=1)

    hits = meta[:, :, :2] == expert.astype(F32)
    taken = jnp.any(hits, axis=2)
    before = jnp.arange(tok)[:, None] > jnp.arange(tok)[None, :]
    slot = jnp.sum(jnp.where(taken[:, :, None, :] & before, 1, 0), axis=3)
    place = taken[:, :, None, :] & (slot[:, :, None, :] == jnp.arange(cap)[:, None])
    tok_weight = jnp.sum(jnp.where(hits, meta[:, :, 2:], 0.0), axis=2)
    scale = jnp.sum(jnp.where(place, tok_weight[:, :, None, :], 0.0), axis=3)
    scale = scale.reshape(2 * rows, 1)

    group = max(1, min(n, 256 // tok))
    eye = jnp.eye(group, dtype=bool)
    wide = place.reshape(2, n // group, group, cap, 1, tok) & eye[:, None, :, None]
    wide = wide.reshape(2 * n // group, group * cap, group * tok).astype(BF)

    def put(tokens):
        routed = lax.dot_general(
            wide,
            tokens.reshape(2 * n // group, group * tok, piece),
            (((2,), (1,)), ((0,), (0,))),
            preferred_element_type=F32,
        ).reshape(2 * rows, piece)
        return routed.astype(BF)

    def times(routed, weight):
        return lax.dot_general(
            routed, weight, (((1,), (1,)), ((), ())), preferred_element_type=F32
        )

    routed_a, routed_b = put(tokens_a), put(tokens_b)
    routed = jnp.concatenate([routed_a, routed_b], axis=1)

    gate = gate_pre[0, 0].astype(F32)
    upper = up_pre[0, 0].astype(F32)
    sig = jax.nn.sigmoid(gate)
    act = gate * sig
    slope = sig * (1.0 + gate * (1.0 - sig))
    hidden = (act * upper).astype(BF)
    hidden_both = jnp.concatenate(ordered(hidden, swap(hidden)), axis=0)

    back = times(routed_a, down_weight[0, :, :piece]) + times(routed_b, down_weight[0, :, piece:])
    back = back.reshape(2, rows, -1)
    sent = lax.dynamic_index_in_dim(back, 1 - me, 0, keepdims=False).astype(BF)
    back = lax.dynamic_index_in_dim(back, me, 0, keepdims=False) + swap(sent).astype(F32)

    scaled = (scale * routed).astype(BF)
    down_grad = lax.dot_general(
        hidden_both, scaled, (((0,), (0,)), ((), ())), preferred_element_type=F32
    ).astype(BF)

    my_scale = lax.dynamic_slice_in_dim(scale, me * rows, rows, 0)
    hidden_grad = my_scale * back
    gate_grad = (hidden_grad * upper * slope).astype(BF)
    up_grad = (hidden_grad * act).astype(BF)
    score = jnp.sum(hidden.astype(F32) * back, axis=1).reshape(n, cap, 1)
    my_place = lax.dynamic_index_in_dim(place, me, 0, keepdims=False)
    my_hits = lax.dynamic_index_in_dim(hits, me, 0, keepdims=False)
    tok_score = jnp.sum(jnp.where(my_place, score, 0.0), axis=1)
    pair = jnp.where(my_hits, tok_score[:, None, :], 0.0)
    pair = lax.all_to_all(pair, ("expert", "tensor"), split_axis=0, concat_axis=0, tiled=True)
    route_grad = jnp.sum(pair, axis=0).T[None]
    return (route_grad, gate_grad[None, None], up_grad[None, None], down_grad[None])


def solution(mesh):
    in_specs = (
        P("dp", ("expert", "tensor"), None),
        P("dp", ("expert", "tensor"), None),
        P("dp", ("expert", "tensor"), None),
        P("dp", "expert", None, "tensor"),
        P("dp", "expert", None, "tensor"),
        P("expert", "tensor", "dp"),
    )
    out_specs = (
        P("dp", ("expert", "tensor"), None),
        P("dp", "expert", None, "tensor"),
        P("dp", "expert", None, "tensor"),
        P("expert", "tensor", "dp"),
    )
    return jax.shard_map(shards, mesh=mesh, in_specs=in_specs, out_specs=out_specs, check_vma=False)
```

```python
import functools

import jax
import jax.numpy as jnp
from jax import lax
from jax.experimental import pallas as pl
from jax.experimental.pallas import tpu as pltpu
from jax.sharding import PartitionSpec as P

BF = jnp.bfloat16
F32 = jnp.float32


def swap(x):
    return lax.ppermute(x, "dp", [(0, 1), (1, 0)])


def gather_kernel(experts, depth, own_ref, out_ref, own_sem, recv_sem, send_sem, x_sem, y_sem):
    expert = lax.axis_index("expert")
    level = lax.axis_index("tensor")
    others = experts // 2 - 1
    a, b = expert // 2, lax.rem(expert, 2)
    x_expert = a * 2 + 1 - b
    y_experts = [lax.rem(a + j, others + 1) * 2 + b for j in range(1, others + 1)]
    partner = {"expert": x_expert, "tensor": level}
    across = [{"expert": e, "tensor": level} for e in y_experts]
    above = {"expert": expert, "tensor": level + 1}
    below = {"expert": expert, "tensor": level - 1}
    has_above, has_below = level < depth - 1, level > 0

    barrier = pltpu.get_barrier_semaphore()

    def greet(target):
        pl.semaphore_signal(barrier, inc=1, device_id=target, device_id_type=pl.DeviceIdType.MESH)

    for target in [partner] + across:
        greet(target)
    pl.when(has_above)(lambda: greet(above))
    pl.when(has_below)(lambda: greet(below))
    ends = jnp.where(has_above, 1, 0) + jnp.where(has_below, 1, 0)
    pl.semaphore_wait(barrier, 1 + others + ends)

    def copy(h, block, target, sem, own=False):
        return pltpu.make_async_remote_copy(
            src_ref=own_ref.at[h] if own else out_ref.at[h, block],
            dst_ref=out_ref.at[h, block],
            send_sem=sem,
            recv_sem=recv_sem.at[h, block],
            device_id=target,
            device_id_type=pl.DeviceIdType.MESH,
        )

    def arrived(h, block):
        copy(h, block, partner, send_sem.at[0, 0, 0]).wait_recv()

    def column(k, up, act):
        t = level - k if up else level + k
        block = expert * depth + t
        own = k == 0

        def go():
            for h in range(2):
                if act == "start" and not own:
                    arrived(h, block)
                todo = []
                if own or up:
                    todo.append((has_above, above, 0))
                if own or not up:
                    todo.append((has_below, below, 1))
                todo.append((None, partner, 2))
                todo += [(None, target, 3 + j) for j, target in enumerate(across)]
                for when, target, kind in todo:
                    one = copy(h, block, target, send_sem.at[h, t, kind], own)
                    run = one.start if act == "start" else one.wait_send
                    if when is None:
                        run()
                    else:
                        pl.when(when)(run)

        pl.when(t >= 0 if up else t < depth)(go)

    def cross(k, up, act):
        t = level - k if up else level + k

        def go():
            block = x_expert * depth + t
            if act == "start":
                arrived(0, block)
            for j, target in enumerate(across):
                one = copy(0, block, target, x_sem.at[t, j])
                one.start() if act == "start" else one.wait_send()
            for j, e in enumerate(y_experts):
                if act == "start":
                    arrived(1, e * depth + t)
                one = copy(1, e * depth + t, partner, y_sem.at[t, j])
                one.start() if act == "start" else one.wait_send()

        pl.when(t >= 0 if up else t < depth)(go)

    mine = expert * depth + level
    keeps = [
        pltpu.make_async_copy(own_ref.at[h], out_ref.at[h, mine], own_sem.at[h]) for h in range(2)
    ]
    for keep in keeps:
        keep.start()
    sides = lambda k: (True,) if k == 0 else (True, False)
    for k in range(depth + 1):
        if k < depth:
            for up in sides(k):
                column(k, up, "start")
        if k > 0:
            for up in sides(k - 1):
                cross(k - 1, up, "start")
    for t in range(depth):
        arrived(1, x_expert * depth + t)
        for e in y_experts:
            arrived(0, e * depth + t)
            far = e + 1 - 2 * b
            arrived(0, far * depth + t)
            arrived(1, far * depth + t)
    for k in range(depth):
        for up in sides(k):
            column(k, up, "end")
            cross(k, up, "end")
    for keep in keeps:
        keep.wait()


def gather(own):
    experts, depth = lax.axis_size("expert"), lax.axis_size("tensor")
    others = experts // 2 - 1
    n = experts * depth
    return pl.pallas_call(
        functools.partial(gather_kernel, experts, depth),
        out_shape=jax.ShapeDtypeStruct((2, n) + own.shape[1:], own.dtype),
        in_specs=[pl.BlockSpec(memory_space=pl.ANY)],
        out_specs=pl.BlockSpec(memory_space=pl.ANY),
        scratch_shapes=[
            pltpu.SemaphoreType.DMA((2,)),
            pltpu.SemaphoreType.DMA((2, n)),
            pltpu.SemaphoreType.DMA((2, depth, 3 + others)),
            pltpu.SemaphoreType.DMA((depth, others)),
            pltpu.SemaphoreType.DMA((depth, others)),
        ],
        compiler_params=pltpu.CompilerParams(collective_id=0, has_side_effects=True),
    )(own)


def shards(out_grad, routes, route_weight, gate_pre, up_pre, down_weight):
    me = lax.axis_index("dp")
    expert = lax.axis_index("expert")
    n = lax.axis_size("expert") * lax.axis_size("tensor")
    rows = gate_pre.shape[2]
    cap = rows // n
    tok, width = out_grad.shape[1:]
    half = width // 2
    first = me == 0

    def ordered(mine, other):
        return jnp.where(first, mine, other), jnp.where(first, other, mine)

    meta = jnp.concatenate([routes[0].astype(BF), route_weight[0]], axis=1)
    meta = jnp.pad(meta, ((0, 0), (0, 124)))
    low = jnp.concatenate([out_grad[0, :, :half], meta], axis=1)
    high = jnp.concatenate([out_grad[0, :, half:], meta], axis=1)
    keep = jnp.where(first, low, high)
    other = swap(jnp.where(first, high, low))
    both = gather(jnp.stack(ordered(keep, other)))
    tokens = both[..., :half]
    meta = jnp.swapaxes(both[..., half : half + 4].astype(F32), 2, 3)

    hits = meta[:, :, :2] == expert.astype(F32)
    taken = jnp.any(hits, axis=2)
    before = jnp.arange(tok)[:, None] > jnp.arange(tok)[None, :]
    slot = jnp.sum(jnp.where(taken[:, :, None, :] & before, 1, 0), axis=3)
    place = taken[:, :, None, :] & (slot[:, :, None, :] == jnp.arange(cap)[:, None])
    tok_weight = jnp.sum(jnp.where(hits, meta[:, :, 2:], 0.0), axis=2)
    scale = jnp.sum(jnp.where(place, tok_weight[:, :, None, :], 0.0), axis=3)
    scale = scale.reshape(2 * rows, 1)

    group = max(1, min(n, 256 // tok))
    eye = jnp.eye(group, dtype=bool)
    wide = place.reshape(2, n // group, group, cap, 1, tok) & eye[:, None, :, None]
    wide = wide.reshape(2 * n // group, group * cap, group * tok).astype(BF)

    routed = lax.dot_general(
        wide,
        tokens.reshape(2 * n // group, group * tok, half),
        (((2,), (1,)), ((0,), (0,))),
        preferred_element_type=F32,
    ).reshape(2 * rows, half)
    routed = routed.astype(BF)

    gate = gate_pre[0, 0].astype(F32)
    upper = up_pre[0, 0].astype(F32)
    sig = jax.nn.sigmoid(gate)
    act = gate * sig
    slope = sig * (1.0 + gate * (1.0 - sig))
    hidden = (act * upper).astype(BF)
    hidden_both = jnp.concatenate(ordered(hidden, swap(hidden)), axis=0)

    back = lax.dot_general(
        routed, down_weight[0], (((1,), (1,)), ((), ())), preferred_element_type=F32
    ).reshape(2, rows, -1)
    sent = lax.dynamic_index_in_dim(back, 1 - me, 0, keepdims=False).astype(BF)
    back = lax.dynamic_index_in_dim(back, me, 0, keepdims=False) + swap(sent).astype(F32)

    scaled = (scale * routed).astype(BF)
    down_grad = lax.dot_general(
        hidden_both, scaled, (((0,), (0,)), ((), ())), preferred_element_type=F32
    ).astype(BF)

    my_scale = lax.dynamic_slice_in_dim(scale, me * rows, rows, 0)
    hidden_grad = my_scale * back
    gate_grad = (hidden_grad * upper * slope).astype(BF)
    up_grad = (hidden_grad * act).astype(BF)
    score = jnp.sum(hidden.astype(F32) * back, axis=1).reshape(n, cap, 1)
    my_place = lax.dynamic_index_in_dim(place, me, 0, keepdims=False)
    my_hits = lax.dynamic_index_in_dim(hits, me, 0, keepdims=False)
    tok_score = jnp.sum(jnp.where(my_place, score, 0.0), axis=1)
    pair = jnp.where(my_hits, tok_score[:, None, :], 0.0)
    pair = lax.all_to_all(pair, ("expert", "tensor"), split_axis=0, concat_axis=0, tiled=True)
    route_grad = jnp.sum(pair, axis=0).T[None]
    return (route_grad, gate_grad[None, None], up_grad[None, None], down_grad[None])


def solution(mesh):
    in_specs = (
        P("dp", ("expert", "tensor"), None),
        P("dp", ("expert", "tensor"), None),
        P("dp", ("expert", "tensor"), None),
        P("dp", "expert", None, "tensor"),
        P("dp", "expert", None, "tensor"),
        P("expert", "tensor", "dp"),
    )
    out_specs = (
        P("dp", ("expert", "tensor"), None),
        P("dp", "expert", None, "tensor"),
        P("dp", "expert", None, "tensor"),
        P("expert", "tensor", "dp"),
    )
    return jax.shard_map(shards, mesh=mesh, in_specs=in_specs, out_specs=out_specs, check_vma=False)
```

```python
import functools

import jax
import jax.numpy as jnp
from jax import lax
from jax.experimental import pallas as pl
from jax.experimental.pallas import tpu as pltpu
from jax.sharding import PartitionSpec as P

BF = jnp.bfloat16
F32 = jnp.float32


def swap(x):
    return lax.ppermute(x, "dp", [(0, 1), (1, 0)])


def gather_kernel(experts, depth, own_ref, out_ref, own_sem, recv_sem, send_sem, x_sem, y_sem):
    expert = lax.axis_index("expert")
    level = lax.axis_index("tensor")
    others = experts // 2 - 1
    a, b = expert // 2, lax.rem(expert, 2)
    x_expert = a * 2 + 1 - b
    y_experts = [lax.rem(a + j, others + 1) * 2 + b for j in range(1, others + 1)]
    partner = {"expert": x_expert, "tensor": level}
    across = [{"expert": e, "tensor": level} for e in y_experts]
    above = {"expert": expert, "tensor": level + 1}
    below = {"expert": expert, "tensor": level - 1}
    has_above, has_below = level < depth - 1, level > 0

    barrier = pltpu.get_barrier_semaphore()

    def greet(target):
        pl.semaphore_signal(barrier, inc=1, device_id=target, device_id_type=pl.DeviceIdType.MESH)

    for target in [partner] + across:
        greet(target)
    pl.when(has_above)(lambda: greet(above))
    pl.when(has_below)(lambda: greet(below))
    ends = jnp.where(has_above, 1, 0) + jnp.where(has_below, 1, 0)
    pl.semaphore_wait(barrier, 1 + others + ends)

    def copy(h, block, target, sem, own=False):
        return pltpu.make_async_remote_copy(
            src_ref=own_ref.at[h] if own else out_ref.at[h, block],
            dst_ref=out_ref.at[h, block],
            send_sem=sem,
            recv_sem=recv_sem.at[h, block],
            device_id=target,
            device_id_type=pl.DeviceIdType.MESH,
        )

    def arrived(h, block):
        copy(h, block, partner, send_sem.at[0, 0, 0]).wait_recv()

    def column(k, up, act):
        t = level - k if up else level + k
        block = expert * depth + t
        own = k == 0

        def go():
            for h in range(2):
                if act == "start" and not own:
                    arrived(h, block)
                todo = []
                if own or up:
                    todo.append((has_above, above, 0))
                if own or not up:
                    todo.append((has_below, below, 1))
                todo.append((None, partner, 2))
                todo += [(None, target, 3 + j) for j, target in enumerate(across)]
                for when, target, kind in todo:
                    one = copy(h, block, target, send_sem.at[h, t, kind], own)
                    run = one.start if act == "start" else one.wait_send
                    if when is None:
                        run()
                    else:
                        pl.when(when)(run)

        pl.when(t >= 0 if up else t < depth)(go)

    def cross(k, up, act):
        t = level - k if up else level + k

        def go():
            block = x_expert * depth + t
            if act == "start":
                arrived(0, block)
            for j, target in enumerate(across):
                one = copy(0, block, target, x_sem.at[t, j])
                one.start() if act == "start" else one.wait_send()
            for j, e in enumerate(y_experts):
                if act == "start":
                    arrived(1, e * depth + t)
                one = copy(1, e * depth + t, partner, y_sem.at[t, j])
                one.start() if act == "start" else one.wait_send()

        pl.when(t >= 0 if up else t < depth)(go)

    mine = expert * depth + level
    keeps = [
        pltpu.make_async_copy(own_ref.at[h], out_ref.at[h, mine], own_sem.at[h]) for h in range(2)
    ]
    for keep in keeps:
        keep.start()
    sides = lambda k: (True,) if k == 0 else (True, False)
    for k in range(depth + 1):
        if k < depth:
            for up in sides(k):
                column(k, up, "start")
        if k > 0:
            for up in sides(k - 1):
                cross(k - 1, up, "start")
    for t in range(depth):
        arrived(1, x_expert * depth + t)
        for e in y_experts:
            arrived(0, e * depth + t)
            far = e + 1 - 2 * b
            arrived(0, far * depth + t)
            arrived(1, far * depth + t)
    for k in range(depth):
        for up in sides(k):
            column(k, up, "end")
            cross(k, up, "end")
    for keep in keeps:
        keep.wait()


def gather(own):
    experts, depth = lax.axis_size("expert"), lax.axis_size("tensor")
    others = experts // 2 - 1
    n = experts * depth
    return pl.pallas_call(
        functools.partial(gather_kernel, experts, depth),
        out_shape=jax.ShapeDtypeStruct((2, n) + own.shape[1:], own.dtype),
        in_specs=[pl.BlockSpec(memory_space=pl.ANY)],
        out_specs=pl.BlockSpec(memory_space=pl.ANY),
        scratch_shapes=[
            pltpu.SemaphoreType.DMA((2,)),
            pltpu.SemaphoreType.DMA((2, n)),
            pltpu.SemaphoreType.DMA((2, depth, 3 + others)),
            pltpu.SemaphoreType.DMA((depth, others)),
            pltpu.SemaphoreType.DMA((depth, others)),
        ],
        compiler_params=pltpu.CompilerParams(collective_id=0, has_side_effects=True),
    )(own)


def place_kernel(wide_ref, tokens_ref, scale_ref, routed_ref, scaled_ref):
    rows = jnp.dot(wide_ref[0], tokens_ref[0], preferred_element_type=F32)
    routed_ref[...] = rows.astype(BF)
    scaled_ref[...] = (scale_ref[...] * rows).astype(BF)


def place_rows(wide, tokens, scale, half):
    groups, rows, toks = wide.shape
    cut = half // 2
    block = pl.BlockSpec((rows, cut), lambda g, j: (g, j))
    return pl.pallas_call(
        place_kernel,
        grid=(groups, 2),
        out_shape=[jax.ShapeDtypeStruct((groups * rows, half), BF)] * 2,
        in_specs=[
            pl.BlockSpec((1, rows, toks), lambda g, j: (g, 0, 0)),
            pl.BlockSpec((1, toks, cut), lambda g, j: (g, 0, j)),
            pl.BlockSpec((rows, 1), lambda g, j: (g, 0)),
        ],
        out_specs=[block, block],
        compiler_params=pltpu.CompilerParams(vmem_limit_bytes=24 * 2**20),
    )(wide, tokens, scale)


def share_sum(x, axis, dim):
    size, index = lax.axis_size(axis), lax.axis_index(axis)
    bit = size // 2
    while bit:
        low, high = jnp.split(x, 2, axis=dim)
        upper = lax.rem(index // bit, 2) == 1
        sent = lax.ppermute(
            jnp.where(upper, low, high), axis, [(i, i ^ bit) for i in range(size)]
        )
        x = jnp.where(upper, high, low) + sent
        bit //= 2
    return x


def shards(out_grad, routes, route_weight, gate_pre, up_pre, down_weight):
    me = lax.axis_index("dp")
    expert = lax.axis_index("expert")
    n = lax.axis_size("expert") * lax.axis_size("tensor")
    rows = gate_pre.shape[2]
    cap = rows // n
    tok, width = out_grad.shape[1:]
    half = width // 2
    first = me == 0

    meta = jnp.concatenate([routes[0].astype(BF), route_weight[0]], axis=1)
    meta = jnp.pad(meta, ((0, 0), (0, 124)))
    low = jnp.concatenate([out_grad[0, :, :half], meta], axis=1)
    high = jnp.concatenate([out_grad[0, :, half:], meta], axis=1)
    keep = jnp.where(first, low, high)
    other = swap(jnp.where(first, high, low))
    both = gather(jnp.stack((keep, other)))
    meta = jnp.swapaxes(both[..., half : half + 4].astype(F32), 2, 3)

    hits = meta[:, :, :2] == expert.astype(F32)
    taken = jnp.any(hits, axis=2)
    before = jnp.arange(tok)[:, None] > jnp.arange(tok)[None, :]
    slot = jnp.sum(jnp.where(taken[:, :, None, :] & before, 1, 0), axis=3)
    place = taken[:, :, None, :] & (slot[:, :, None, :] == jnp.arange(cap)[:, None])
    tok_weight = jnp.sum(jnp.where(hits, meta[:, :, 2:], 0.0), axis=2)
    scale = jnp.sum(jnp.where(place, tok_weight[:, :, None, :], 0.0), axis=3)
    scale = scale.reshape(2 * rows, 1)

    group = max(1, min(n, 256 // tok))
    eye = jnp.eye(group, dtype=bool)
    wide = place.reshape(2, n // group, group, cap, 1, tok) & eye[:, None, :, None]
    wide = wide.reshape(2 * n // group, group * cap, group * tok).astype(BF)

    routed, scaled = place_rows(
        wide, both.reshape(2 * n // group, group * tok, half + 128), scale, half
    )

    gate = gate_pre[0, 0].astype(F32)
    upper = up_pre[0, 0].astype(F32)
    sig = jax.nn.sigmoid(gate)
    act = gate * sig
    slope = sig * (1.0 + gate * (1.0 - sig))
    hidden = (act * upper).astype(BF)
    hidden_both = jnp.concatenate((hidden, swap(hidden)), axis=0)

    back = lax.dot_general(
        routed, down_weight[0], (((1,), (1,)), ((), ())), preferred_element_type=F32
    ).reshape(2, rows, -1)
    back = back[0] + swap(back[1].astype(BF)).astype(F32)

    down_grad = lax.dot_general(
        hidden_both, scaled, (((0,), (0,)), ((), ())), preferred_element_type=F32
    ).astype(BF)

    my_scale = scale[:rows]
    hidden_grad = my_scale * back
    gate_grad = (hidden_grad * upper * slope).astype(BF)
    up_grad = (hidden_grad * act).astype(BF)
    score = jnp.sum(hidden.astype(F32) * back, axis=1).reshape(n, cap, 1)
    tok_score = jnp.sum(jnp.where(place[0], score, 0.0), axis=1)
    pair = jnp.where(hits[0], tok_score[:, None, :], 0.0)
    pair = pair.reshape(lax.axis_size("expert"), lax.axis_size("tensor"), 2, tok)
    pair = share_sum(share_sum(pair, "tensor", 1), "expert", 0)
    route_grad = pair.reshape(2, tok).T[None]
    return (route_grad, gate_grad[None, None], up_grad[None, None], down_grad[None])


def solution(mesh):
    in_specs = (
        P("dp", ("expert", "tensor"), None),
        P("dp", ("expert", "tensor"), None),
        P("dp", ("expert", "tensor"), None),
        P("dp", "expert", None, "tensor"),
        P("dp", "expert", None, "tensor"),
        P("expert", "tensor", "dp"),
    )
    out_specs = (
        P("dp", ("expert", "tensor"), None),
        P("dp", "expert", None, "tensor"),
        P("dp", "expert", None, "tensor"),
        P("expert", "tensor", "dp"),
    )
    return jax.shard_map(shards, mesh=mesh, in_specs=in_specs, out_specs=out_specs, check_vma=False)
```

```python
import functools

import jax
import jax.numpy as jnp
from jax import lax
from jax.experimental import pallas as pl
from jax.experimental.pallas import tpu as pltpu
from jax.sharding import PartitionSpec as P

BF = jnp.bfloat16
F32 = jnp.float32


def swap(x):
    return lax.ppermute(x, "dp", [(0, 1), (1, 0)])


def gather_kernel(experts, depth, own_ref, out_ref, own_sem, recv_sem, send_sem, x_sem, y_sem):
    expert = lax.axis_index("expert")
    level = lax.axis_index("tensor")
    others = experts // 2 - 1
    a, b = expert // 2, lax.rem(expert, 2)
    x_expert = a * 2 + 1 - b
    y_experts = [lax.rem(a + j, others + 1) * 2 + b for j in range(1, others + 1)]
    partner = {"expert": x_expert, "tensor": level}
    across = [{"expert": e, "tensor": level} for e in y_experts]
    above = {"expert": expert, "tensor": level + 1}
    below = {"expert": expert, "tensor": level - 1}
    has_above, has_below = level < depth - 1, level > 0

    barrier = pltpu.get_barrier_semaphore()

    def greet(target):
        pl.semaphore_signal(barrier, inc=1, device_id=target, device_id_type=pl.DeviceIdType.MESH)

    for target in [partner] + across:
        greet(target)
    pl.when(has_above)(lambda: greet(above))
    pl.when(has_below)(lambda: greet(below))
    ends = jnp.where(has_above, 1, 0) + jnp.where(has_below, 1, 0)
    pl.semaphore_wait(barrier, 1 + others + ends)

    def copy(h, block, target, sem, own=False):
        return pltpu.make_async_remote_copy(
            src_ref=own_ref.at[h] if own else out_ref.at[h, block],
            dst_ref=out_ref.at[h, block],
            send_sem=sem,
            recv_sem=recv_sem.at[h, block],
            device_id=target,
            device_id_type=pl.DeviceIdType.MESH,
        )

    def arrived(h, block):
        copy(h, block, partner, send_sem.at[0, 0, 0]).wait_recv()

    def column(k, up, act):
        t = level - k if up else level + k
        block = expert * depth + t
        own = k == 0

        def go():
            for h in range(2):
                if act == "start" and not own:
                    arrived(h, block)
                todo = []
                if own or up:
                    todo.append((has_above, above, 0))
                if own or not up:
                    todo.append((has_below, below, 1))
                todo.append((None, partner, 2))
                todo += [(None, target, 3 + j) for j, target in enumerate(across)]
                for when, target, kind in todo:
                    one = copy(h, block, target, send_sem.at[h, t, kind], own)
                    run = one.start if act == "start" else one.wait_send
                    if when is None:
                        run()
                    else:
                        pl.when(when)(run)

        pl.when(t >= 0 if up else t < depth)(go)

    def cross(k, up, act):
        t = level - k if up else level + k

        def go():
            block = x_expert * depth + t
            if act == "start":
                arrived(0, block)
            for j, target in enumerate(across):
                one = copy(0, block, target, x_sem.at[t, j])
                one.start() if act == "start" else one.wait_send()
            for j, e in enumerate(y_experts):
                if act == "start":
                    arrived(1, e * depth + t)
                one = copy(1, e * depth + t, partner, y_sem.at[t, j])
                one.start() if act == "start" else one.wait_send()

        pl.when(t >= 0 if up else t < depth)(go)

    mine = expert * depth + level
    keeps = [
        pltpu.make_async_copy(own_ref.at[h], out_ref.at[h, mine], own_sem.at[h]) for h in range(2)
    ]
    for keep in keeps:
        keep.start()
    sides = lambda k: (True,) if k == 0 else (True, False)
    for k in range(depth + 1):
        if k < depth:
            for up in sides(k):
                column(k, up, "start")
        if k > 0:
            for up in sides(k - 1):
                cross(k - 1, up, "start")
    for t in range(depth):
        arrived(1, x_expert * depth + t)
        for e in y_experts:
            arrived(0, e * depth + t)
            far = e + 1 - 2 * b
            arrived(0, far * depth + t)
            arrived(1, far * depth + t)
    for k in range(depth):
        for up in sides(k):
            column(k, up, "end")
            cross(k, up, "end")
    for keep in keeps:
        keep.wait()


def gather(own):
    experts, depth = lax.axis_size("expert"), lax.axis_size("tensor")
    others = experts // 2 - 1
    n = experts * depth
    return pl.pallas_call(
        functools.partial(gather_kernel, experts, depth),
        out_shape=jax.ShapeDtypeStruct((2, n) + own.shape[1:], own.dtype),
        in_specs=[pl.BlockSpec(memory_space=pl.ANY)],
        out_specs=pl.BlockSpec(memory_space=pl.ANY),
        scratch_shapes=[
            pltpu.SemaphoreType.DMA((2,)),
            pltpu.SemaphoreType.DMA((2, n)),
            pltpu.SemaphoreType.DMA((2, depth, 3 + others)),
            pltpu.SemaphoreType.DMA((depth, others)),
            pltpu.SemaphoreType.DMA((depth, others)),
        ],
        compiler_params=pltpu.CompilerParams(collective_id=0, has_side_effects=True),
    )(own)


def place_kernel(wide_ref, tokens_ref, scale_ref, routed_ref, scaled_ref):
    rows = jnp.dot(wide_ref[0], tokens_ref[0], preferred_element_type=F32)
    routed_ref[...] = rows.astype(BF)
    scaled_ref[...] = (scale_ref[...] * rows).astype(BF)


def place_rows(wide, tokens, scale, half):
    groups, rows, toks = wide.shape
    cut = half // 2
    block = pl.BlockSpec((rows, cut), lambda g, j: (g, j))
    return pl.pallas_call(
        place_kernel,
        grid=(groups, 2),
        out_shape=[jax.ShapeDtypeStruct((groups * rows, half), BF)] * 2,
        in_specs=[
            pl.BlockSpec((1, rows, toks), lambda g, j: (g, 0, 0)),
            pl.BlockSpec((1, toks, cut), lambda g, j: (g, 0, j)),
            pl.BlockSpec((rows, 1), lambda g, j: (g, 0)),
        ],
        out_specs=[block, block],
        compiler_params=pltpu.CompilerParams(vmem_limit_bytes=24 * 2**20),
    )(wide, tokens, scale)


def shards(out_grad, routes, route_weight, gate_pre, up_pre, down_weight):
    me = lax.axis_index("dp")
    expert = lax.axis_index("expert")
    n = lax.axis_size("expert") * lax.axis_size("tensor")
    rows = gate_pre.shape[2]
    cap = rows // n
    tok, width = out_grad.shape[1:]
    half = width // 2
    first = me == 0

    meta = jnp.concatenate([routes[0].astype(BF), route_weight[0]], axis=1)
    meta = jnp.pad(meta, ((0, 0), (0, 124)))
    low = jnp.concatenate([out_grad[0, :, :half], meta], axis=1)
    high = jnp.concatenate([out_grad[0, :, half:], meta], axis=1)
    keep = jnp.where(first, low, high)
    other = swap(jnp.where(first, high, low))
    both = gather(jnp.stack((keep, other)))
    meta = jnp.swapaxes(both[..., half : half + 4].astype(F32), 2, 3)

    hits = meta[:, :, :2] == expert.astype(F32)
    taken = jnp.any(hits, axis=2)
    before = jnp.arange(tok)[:, None] > jnp.arange(tok)[None, :]
    slot = jnp.sum(jnp.where(taken[:, :, None, :] & before, 1, 0), axis=3)
    place = taken[:, :, None, :] & (slot[:, :, None, :] == jnp.arange(cap)[:, None])
    tok_weight = jnp.sum(jnp.where(hits, meta[:, :, 2:], 0.0), axis=2)
    scale = jnp.sum(jnp.where(place, tok_weight[:, :, None, :], 0.0), axis=3)
    scale = scale.reshape(2 * rows, 1)

    group = max(1, min(n, 256 // tok))
    eye = jnp.eye(group, dtype=bool)
    wide = place.reshape(2, n // group, group, cap, 1, tok) & eye[:, None, :, None]
    wide = wide.reshape(2 * n // group, group * cap, group * tok).astype(BF)

    routed, scaled = place_rows(
        wide, both.reshape(2 * n // group, group * tok, half + 128), scale, half
    )

    gate = gate_pre[0, 0].astype(F32)
    upper = up_pre[0, 0].astype(F32)
    sig = jax.nn.sigmoid(gate)
    act = gate * sig
    slope = sig * (1.0 + gate * (1.0 - sig))
    hidden = (act * upper).astype(BF)
    hidden_both = jnp.concatenate((hidden, swap(hidden)), axis=0)

    back = lax.dot_general(
        routed, down_weight[0], (((1,), (1,)), ((), ())), preferred_element_type=F32
    ).reshape(2, rows, -1)
    back = back[0] + swap(back[1].astype(BF)).astype(F32)

    down_grad = lax.dot_general(
        hidden_both, scaled, (((0,), (0,)), ((), ())), preferred_element_type=F32
    ).astype(BF)

    my_scale = scale[:rows]
    hidden_grad = my_scale * back
    gate_grad = (hidden_grad * upper * slope).astype(BF)
    up_grad = (hidden_grad * act).astype(BF)
    score = jnp.sum(hidden.astype(F32) * back, axis=1).reshape(n, cap, 1)
    tok_score = jnp.sum(jnp.where(place[0], score, 0.0), axis=1)
    pair = jnp.where(hits[0], tok_score[:, None, :], 0.0)
    pair = lax.all_to_all(pair, ("expert", "tensor"), split_axis=0, concat_axis=0, tiled=True)
    route_grad = jnp.sum(pair, axis=0).T[None]
    return (route_grad, gate_grad[None, None], up_grad[None, None], down_grad[None])


def solution(mesh):
    in_specs = (
        P("dp", ("expert", "tensor"), None),
        P("dp", ("expert", "tensor"), None),
        P("dp", ("expert", "tensor"), None),
        P("dp", "expert", None, "tensor"),
        P("dp", "expert", None, "tensor"),
        P("expert", "tensor", "dp"),
    )
    out_specs = (
        P("dp", ("expert", "tensor"), None),
        P("dp", "expert", None, "tensor"),
        P("dp", "expert", None, "tensor"),
        P("expert", "tensor", "dp"),
    )
    return jax.shard_map(shards, mesh=mesh, in_specs=in_specs, out_specs=out_specs, check_vma=False)
```
